128 devices in a mesh: blk: 8 (over z_lo, y), width: 16 (over z_hi, x, core).
Axes of the slice: x: 4, y: 4, z: 4 (z_hi: 2, z_lo: 2; z = z_hi * 2 + z_lo), core: 2. Of those that a mesh axis runs over, the one named last changes fastest.
Arguments:
- tokens: bfloat16 [4096, 4096], P('blk', 'width'), may hold values from -96 to 96
- gates: float32 [16, 8], P('blk'), may hold values from 0 to 1, as said below
- w_gate: bfloat16 [8, 4096, 7168], P(None, 'width', 'blk'), may hold values from -0.25 to 0.25
- w_up: bfloat16 [8, 4096, 7168], P(None, 'width', 'blk'), may hold values from -0.25 to 0.25
- w_down: bfloat16 [8, 7168, 4096], P(None, 'blk', 'width'), may hold values from -0.21875 to 0.21875
Outputs:
- mixed: bfloat16 [4096, 4096], P('blk', 'width')
The draws below stay inside these ranges and needn't reach their ends.
Inputs may be any that keep to these rules, and one draw needn't show every extreme that they name: Each row of gates is the first 8 entries of a softmax over 16 experts: positive, summing to less than 1.
All inputs are finite; a program needn't handle non-finite values.
Results may differ from the reference program's by a relative error of at most 0.034.
Values may be sent and summed in bfloat16 or wider, within the bound.
A program may use at most 128 MiB of HBM per device.

```python
import math
import jax
import jax.numpy as jnp
from jax import lax

D = 4096
FF = 7168
E = 8
SEG = 256
SEGS = 16
N_WIDTH = 16


def segment_levels(key):
    level_key = jax.random.fold_in(key, 7)
    spread_key, strong_key, offset_key, faint_key = jax.random.split(level_key, 4)
    levels = jnp.exp(jax.random.uniform(spread_key, (SEGS,), jnp.float32, math.log(0.1), 0.0))
    strongest = jax.random.randint(strong_key, (), 0, SEGS)
    weakest = (strongest + jax.random.randint(offset_key, (), 1, SEGS)) % SEGS
    faintest = 0.1 * jnp.exp(jax.random.uniform(faint_key, (), jnp.float32, 0.0, math.log(1.1)))
    segment_index = jnp.arange(SEGS)
    levels = jnp.where(segment_index == strongest, jnp.float32(1.0), levels)
    levels = jnp.where(segment_index == weakest, faintest, levels)
    return levels


def draw_gates(key, part):
    levels = segment_levels(key)
    logits = jax.random.normal(jax.random.fold_in(key, 13), (SEGS, E), jnp.float32)
    logits = logits * 1.5
    shares = jax.nn.softmax(logits, axis=-1)
    length = jnp.sqrt(jnp.sum(shares * shares, axis=-1, keepdims=True))
    weights = 0.9 / math.sqrt(E) * levels[:, None] * shares / length
    return weights.astype(jnp.float32)


def draw_tokens(key, part):
    levels = segment_levels(key)
    factor = 0.5 * levels ** (-1.5)
    noise_key = jax.random.fold_in(key, 29)
    values = jnp.clip(jax.random.normal(noise_key, (SEGS, SEG, D), jnp.float32), -6.0, 6.0)
    values = values * factor[:, None, None]
    return values.reshape(SEGS * SEG, D).astype(jnp.bfloat16)


def block_scale(key, dims, shards, smallest, top_value):
    def one(axis_at, shards_of):
        steps = jax.random.uniform(jax.random.fold_in(jax.random.fold_in(key, 6), axis_at), (shards_of,), jnp.float32, smallest / len(shards), top_value / len(shards))
        return jnp.repeat(jnp.exp(steps), dims[axis_at] // shards_of).reshape((-1,) + (1,) * (len(dims) - axis_at - 1))

    loudness = one(*shards[0])
    for cut in shards[1:]:
        loudness = loudness * one(*cut)
    return loudness


def bell_draw(key, dims, spread, bound, cuts=(), dtype=jnp.bfloat16):
    gain = block_scale(key, dims, cuts, -0.22, 0.18) if cuts else 1.0
    drawn = jax.random.normal(key, dims, jnp.float32) * spread * gain
    return jnp.minimum(jnp.maximum(drawn, -bound), bound).astype(dtype)


def setup_inputs(seed: int = 0) -> dict:
    key_of = jax.random.split(jax.random.key(seed), 6)
    return {
        "tokens": draw_tokens(jax.random.fold_in(key_of[5], 71), 0),
        "gates": draw_gates(jax.random.fold_in(key_of[5], 71), 0),
        "w_gate": bell_draw(key_of[2], (E, D, FF), (3.0 * D ** -0.5), 0.25, ((1, 16), (2, 8))),
        "w_up": bell_draw(key_of[3], (E, D, FF), (3.0 * D ** -0.5), 0.25, ((1, 16), (2, 8))),
        "w_down": bell_draw(key_of[4], (E, FF, D), (3.0 * FF ** -0.5), 0.21875, ((1, 8), (2, 16))),
    }


def merge(weights_row, stack):
    total = jnp.zeros(stack.shape[1:], jnp.float32)
    for expert in range(E):
        total = total + weights_row[expert] * stack[expert].astype(jnp.float32)
    return total.astype(jnp.bfloat16)


def reference(tokens, gates, w_gate, w_up, w_down):
    blocks = N_WIDTH
    block_width = D // blocks
    segments = tokens.reshape(SEGS, SEG, D)

    def one_segment(pair):
        seg_rows, weights_row = pair
        merged_gate = merge(weights_row, w_gate)
        merged_up = merge(weights_row, w_up)
        merged_down = merge(weights_row, w_down)

        def partial_total(merged):
            left = seg_rows.reshape(SEG, blocks, block_width).astype(jnp.float32)
            right = merged.reshape(blocks, block_width, FF).astype(jnp.float32)
            parts = jnp.einsum('tkd,kdf->ktf', left, right)
            rounded = lax.optimization_barrier(parts.astype(jnp.bfloat16))
            return jnp.sum(rounded.astype(jnp.float32), axis=0)

        gate_sum = partial_total(merged_gate)
        up_sum = partial_total(merged_up)
        hidden = (jax.nn.silu(gate_sum) * up_sum).astype(jnp.bfloat16)
        return jnp.dot(hidden, merged_down, preferred_element_type=jnp.float32).astype(jnp.bfloat16)

    mixed = lax.map(one_segment, (segments, gates))
    return mixed.reshape(SEGS * SEG, D)
```

```python
import functools
import jax
import jax.numpy as jnp
from jax import lax
from jax.experimental import pallas as pl
from jax.experimental.pallas import tpu as pltpu
from jax.sharding import PartitionSpec as P

SEG = 256
EXPERTS = 8
UNITS = 16
SUB = 32
TILE = 256
SLOTS = 4
MESH = pl.DeviceIdType.MESH
OFFSETS = (0, 1, 6, 9, 12, 15, 18, 22, 23)


def kernel(
    gates_ref, tokens_ref, wg_ref, wu_ref, wd_ref, out_ref,
    gbuf, kmat, keep, psend, precv, r1, r2, r3, merged, wdn, tok, hid, term, yrecv, zsend, zrecv,
    w_sem, l_sem, g_s, g_r, tok_s, tok_r, rs_s, rs_r, ag_s, ag_r, t_s, t_r, z_s, z_r,
):
    depth = tokens_ref.shape[1]
    ff = wg_ref.shape[2]
    cols = 2 * ff
    half, quarter, eighth, share = SEG // 2, SEG // 4, SEG // 8, SEG // 16

    w = lax.axis_index("width")
    b = lax.axis_index("blk")
    core = lax.rem(w, 2)
    x = lax.rem(w // 2, 4)
    zh = w // 8
    y = lax.rem(b, 4)
    zl = b // 4

    bit_a, bit_b = lax.rem((x + 1) // 2, 2), x // 2
    w_pair = w + 1 - 2 * core
    w_a = (zh * 4 + x + 1 - 2 * lax.rem(x, 2)) * 2 + core
    w_b = (zh * 4 + 3 - x) * 2 + core
    w_z = ((1 - zh) * 4 + x) * 2 + core
    b_z = (1 - zl) * 4 + y

    def mul(value, by):
        return pl.multiple_of(value, by)

    def dim(u, place):
        d = lax.rem(u + place, 3)
        e0, e1, e2 = (2 - d) * (1 - d) // 2, d * (2 - d), d * (d - 1) // 2
        return e0 * bit_a + e1 * bit_b + e2 * zh, e0 * w_a + e1 * w_b + e2 * w_z

    def place_of(u):
        r, j = u // 2, lax.rem(u, 2)
        q = lax.rem(r, 4)
        dy = lax.rem(1 + 2 * q + q // 2, 4)
        dz = lax.rem((r + 1) // 4, 2)
        zo = zl + dz - 2 * zl * dz
        owner = zo * 4 + lax.rem(y + dy, 4)
        return dy, owner, owner * 2 + j

    def rcopy(src, dst, send, recv, device):
        return pltpu.make_async_remote_copy(
            src_ref=src, dst_ref=dst, send_sem=send, recv_sem=recv, device_id=device, device_id_type=MESH
        )

    def weight_copies(i):
        rows = pl.ds(mul(i * SUB, SUB), SUB)
        return (
            pltpu.make_async_copy(wg_ref.at[:, rows, :], keep.at[:, rows, pl.ds(0, ff)], w_sem.at[0, i]),
            pltpu.make_async_copy(wu_ref.at[:, rows, :], keep.at[:, rows, pl.ds(ff, ff)], w_sem.at[1, i]),
        )

    own_tok = [
        pltpu.make_async_copy(tokens_ref.at[pl.ds(j * SEG, SEG), :], tok.at[2 * b + j], l_sem.at[j])
        for j in range(2)
    ]
    down_copy = pltpu.make_async_copy(wd_ref, wdn, l_sem.at[2])

    for copy in own_tok:
        copy.start()

    @pl.loop(0, depth // SUB)
    def _(i):
        for copy in weight_copies(i):
            copy.start()

    down_copy.start()

    gbuf[b] = jnp.zeros((8, 128), jnp.float32)
    gbuf[b, 0:2, 0:EXPERTS] = gates_ref[...]

    barrier = pltpu.get_barrier_semaphore()
    for partner in (w_pair, w_a, w_b, w_z):
        pl.semaphore_signal(barrier, inc=1, device_id=(b, partner), device_id_type=MESH)
    for p in range(1, 8):
        pl.semaphore_signal(barrier, inc=1, device_id=(lax.rem(b + p, 8), w), device_id_type=MESH)
    pl.semaphore_wait(barrier, 11)

    def gate_copy(p):
        return rcopy(gbuf.at[b], gbuf.at[b], g_s.at[p], g_r.at[p], (lax.rem(b + p, 8), w))

    def gate_arrival(p):
        src = lax.rem(b + 8 - p, 8)
        return rcopy(gbuf.at[src], gbuf.at[src], g_s.at[p], g_r.at[p], (lax.rem(b + p, 8), w))

    for p in range(1, 8):
        gate_copy(p).start()

    def tok_copy(k, source, target):
        block = tok.at[pl.ds(2 * source, 2)]
        return rcopy(block, block, tok_s.at[k], tok_r.at[source], (target, w))

    def y_block(dy):
        return zl * 4 + lax.rem(y + dy, 4)

    for copy in own_tok:
        copy.wait()
    tok_copy(0, b, b_z).start()
    for k, dy in enumerate((3, 1, 2)):
        tok_copy(1 + k, b, y_block(dy)).start()

    for p in range(1, 8):
        gate_arrival(p).wait_recv()
    rows_k, cols_k = UNITS * SUB, EXPERTS * SUB
    shift = SUB.bit_length() - 1
    row = lax.broadcasted_iota(jnp.int32, (rows_k, 64), 0) >> shift
    col = lax.broadcasted_iota(jnp.int32, (rows_k, 64), 1)
    pick_row = ((row >> 1) * 8 + (row & 1) == col).astype(jnp.float32).astype(jnp.bfloat16)
    pick_col = (
        (lax.broadcasted_iota(jnp.int32, (128, cols_k), 1) >> shift)
        == lax.broadcasted_iota(jnp.int32, (128, cols_k), 0)
    ).astype(jnp.float32).astype(jnp.bfloat16)
    weights = gbuf[...].reshape(64, 128).astype(jnp.bfloat16)
    spread = jnp.dot(pick_row, weights, preferred_element_type=jnp.float32).astype(jnp.bfloat16)
    spread = jnp.dot(spread, pick_col, preferred_element_type=jnp.float32)
    same = (lax.broadcasted_iota(jnp.int32, (rows_k, cols_k), 0) & (SUB - 1)) == (
        lax.broadcasted_iota(jnp.int32, (rows_k, cols_k), 1) & (SUB - 1)
    )
    kmat[...] = jnp.where(same, spread, 0.0).astype(jnp.bfloat16)

    @pl.loop(0, depth // SUB)
    def _(i):
        for copy in weight_copies(i):
            copy.wait()
        rows = pl.ds(mul(i * SUB, SUB), SUB)
        for n in range(cols // TILE):
            experts = keep[:, rows, n * TILE : (n + 1) * TILE].reshape(cols_k, TILE)
            total = jnp.dot(kmat[...], experts, preferred_element_type=jnp.float32)
            merged[:, n, rows, :] = total.astype(jnp.bfloat16).reshape(UNITS, SUB, TILE)

    tok_copy(0, b_z, b_z).wait_recv()
    for k, dy in enumerate((3, 1, 2)):
        tok_copy(4 + k, b_z, y_block(dy)).start()

    def kept(u, offset, count):
        return keep.at[u // 2, pl.ds(mul(lax.rem(u, 2) * half + offset, 16), count), :]

    def reduce_copy(u, stage):
        if stage == 0:
            return rcopy(psend.at[lax.rem(u, SLOTS)], precv.at[u], rs_s.at[0, u], rs_r.at[0, u], (b, w_pair))
        (b1, w1), (b2, w2), (b3, w3) = (dim(u, k) for k in range(3))
        if stage == 1:
            return rcopy(kept(u, (1 - b1) * quarter, quarter), r1.at[u], rs_s.at[1, u], rs_r.at[1, u], (b, w1))
        if stage == 2:
            offset = b1 * quarter + (1 - b2) * eighth
            return rcopy(kept(u, offset, eighth), r2.at[u], rs_s.at[2, u], rs_r.at[2, u], (b, w2))
        offset = b1 * quarter + b2 * eighth + (1 - b3) * share
        return rcopy(kept(u, offset, share), r3.at[u], rs_s.at[3, u], rs_r.at[3, u], (b, w3))

    def gather_copy(u, stage):
        (b1, w1), (b2, w2), (b3, w3) = (dim(u, k) for k in range(3))
        offset = core * half
        if stage < 3:
            offset = offset + b1 * quarter
        if stage < 2:
            offset = offset + b2 * eighth
        if stage < 1:
            offset = offset + b3 * share
        count = share << stage
        block = hid.at[u, pl.ds(mul(offset, 16), count), :]
        target = (w3, w2, w1, w_pair)[stage]
        return rcopy(block, block, ag_s.at[stage, u], ag_r.at[stage, u], (b, target))

    def gather_arrival(u, stage):
        (b1, w1), (b2, w2), (b3, w3) = (dim(u, k) for k in range(3))
        offset = core * half if stage < 3 else (1 - core) * half
        if stage < 3:
            offset = offset + (b1 if stage < 2 else 1 - b1) * quarter
        if stage < 2:
            offset = offset + (b2 if stage < 1 else 1 - b2) * eighth
        if stage < 1:
            offset = offset + (1 - b3) * share
        count = share << stage
        block = hid.at[u, pl.ds(mul(offset, 16), count), :]
        target = (w3, w2, w1, w_pair)[stage]
        return rcopy(block, block, ag_s.at[stage, u], ag_r.at[stage, u], (b, target))

    def term_copy(u):
        dy, owner, _ = place_of(u)
        return rcopy(term.at[u], yrecv.at[u], t_s.at[u], t_r.at[u], (y_block(dy), w))

    def f32(block):
        return block.astype(jnp.float32)

    def project(u):
        _, owner, s = place_of(u)

        @pl.when((lax.rem(u, 2) == 0) & (u != 6) & (u != 14))
        def _():
            tok_copy(0, owner, b_z).wait_recv()

        @pl.when(u >= SLOTS)
        def _():
            reduce_copy(u - SLOTS, 0).wait_send()

        rows = jnp.concatenate(
            [tok[s, pl.ds(mul(core * half, half), half), :], tok[s, pl.ds(mul((1 - core) * half, half), half), :]],
            axis=0,
        )
        slot = lax.rem(u, SLOTS)
        mine = pl.ds(mul(lax.rem(u, 2) * half, half), half)
        for n in range(cols // TILE):
            part = jnp.dot(rows, merged[s, n], preferred_element_type=jnp.float32).astype(jnp.bfloat16)
            keep[u // 2, mine, n * TILE : (n + 1) * TILE] = part[:half]
            psend[slot, :, n * TILE : (n + 1) * TILE] = part[half:]
        reduce_copy(u, 0).start()

    def reduce_1(u):
        reduce_copy(u, 0).wait_recv()
        b1, _ = dim(u, 0)
        base = lax.rem(u, 2) * half
        for i in range(quarter // 16):
            offset = (1 - b1) * quarter + i * 16
            at = pl.ds(mul(base + offset, 16), 16)
            total = f32(keep[u // 2, at, :]) + f32(precv[u, pl.ds(mul(offset, 16), 16), :])
            keep[u // 2, at, :] = total.astype(jnp.bfloat16)
        reduce_copy(u, 1).start()

    def reduce_2(u):
        reduce_copy(u, 1).wait_recv()
        (b1, _), (b2, _) = dim(u, 0), dim(u, 1)
        base = lax.rem(u, 2) * half
        for i in range(eighth // 16):
            inner = (1 - b2) * eighth + i * 16
            offset = b1 * quarter + inner
            at = pl.ds(mul(base + offset, 16), 16)
            total = (
                f32(keep[u // 2, at, :])
                + f32(precv[u, pl.ds(mul(offset, 16), 16), :])
                + f32(r1[u, pl.ds(mul(inner, 16), 16), :])
            )
            keep[u // 2, at, :] = total.astype(jnp.bfloat16)
        reduce_copy(u, 2).start()

    def gathered(u, last):
        (b1, _), (b2, _) = dim(u, 0), dim(u, 1)
        base = lax.rem(u, 2) * half
        inner = b2 * eighth + last * share
        offset = b1 * quarter + inner
        return pl.ds(mul(base + offset, 16), 16), (
            f32(keep[u // 2, pl.ds(mul(base + offset, 16), 16), :])
            + f32(precv[u, pl.ds(mul(offset, 16), 16), :])
            + f32(r1[u, pl.ds(mul(inner, 16), 16), :])
            + f32(r2[u, pl.ds(mul(last * share, 16), 16), :])
        )

    def reduce_3(u):
        reduce_copy(u, 2).wait_recv()
        b3, _ = dim(u, 2)
        at, total = gathered(u, 1 - b3)
        keep[u // 2, at, :] = total.astype(jnp.bfloat16)
        reduce_copy(u, 3).start()

    def activate(u):
        reduce_copy(u, 3).wait_recv()
        (b1, _), (b2, _), (b3, _) = (dim(u, k) for k in range(3))
        _, total = gathered(u, b3)
        total = total + f32(r3[u])
        gate, up = total[:, :ff], total[:, ff:]
        value = (gate / (1.0 + jnp.exp(-gate)) * up).astype(jnp.bfloat16)
        offset = core * half + b1 * quarter + b2 * eighth + b3 * share
        hid[u, pl.ds(mul(offset, 16), 16), :] = value
        gather_copy(u, 0).start()

    def spread_on(stage):
        def run(u):
            gather_arrival(u, stage - 1).wait_recv()
            gather_copy(u, stage).start()

        return run

    def finish(u):
        gather_arrival(u, 3).wait_recv()
        dy, _, s = place_of(u)
        down = merged[s, 0:4].reshape(4 * TILE, TILE)[:ff]
        part = jnp.dot(hid[u], down, preferred_element_type=jnp.float32)
        term[u] = part.astype(jnp.bfloat16)

        @pl.when(dy != 0)
        def _():
            term_copy(u).start()

    def merge_down(i):
        rows = pl.ds(mul(i * SUB, SUB), SUB)
        experts = wdn[:, rows, :].reshape(cols_k, TILE)
        total = jnp.dot(kmat[...], experts, preferred_element_type=jnp.float32)
        to = pl.ds(mul(lax.rem(i, TILE // SUB) * SUB, SUB), SUB)
        merged[:, i // (TILE // SUB), to, :] = total.astype(jnp.bfloat16).reshape(UNITS, SUB, TILE)

    def z_copy(j):
        return rcopy(zsend.at[j], zrecv.at[j], z_s.at[j], z_r.at[j], (b_z, w))

    def send_z():
        for j in range(2):
            total = f32(term[6 + j])
            for r in (4, 5, 6):
                term_copy(2 * r + j).wait_recv()
                total = total + f32(yrecv[2 * r + j])
            zsend[j] = total.astype(jnp.bfloat16)
            z_copy(j).start()

    stages = (
        project, reduce_1, reduce_2, reduce_3, activate,
        spread_on(1), spread_on(2), spread_on(3), finish,
    )
    down_steps = OFFSETS[8] - UNITS
    per_step = -(-(ff // SUB) // down_steps)

    @pl.loop(0, UNITS + OFFSETS[8])
    def _(t):
        for stage, offset in zip(stages, OFFSETS):
            @pl.when((t >= offset) & (t < offset + UNITS))
            def _():
                stage(t - offset)

        @pl.when(t == UNITS)
        def _():
            down_copy.wait()

        @pl.when((t >= UNITS) & (t < OFFSETS[8]))
        def _():
            @pl.loop(0, per_step)
            def _(k):
                i = (t - UNITS) * per_step + k

                @pl.when(i < ff // SUB)
                def _():
                    merge_down(i)

        @pl.when(t == OFFSETS[8] + 14)
        def _():
            send_z()

    for j in range(2):
        total = f32(term[14 + j])
        for r in (0, 1, 2):
            term_copy(2 * r + j).wait_recv()
            total = total + f32(yrecv[2 * r + j])
        z_copy(j).wait_recv()
        total = total + f32(zrecv[j])
        out_ref[j * SEG : (j + 1) * SEG, :] = total.astype(jnp.bfloat16)

    for p in range(1, 8):
        gate_copy(p).wait_send()
    tok_copy(0, b, b_z).wait_send()
    for k, dy in enumerate((3, 1, 2)):
        tok_copy(1 + k, b, y_block(dy)).wait_send()
        tok_copy(4 + k, b_z, y_block(dy)).wait_send()

    @pl.loop(0, UNITS)
    def _(u):
        @pl.when(u >= UNITS - SLOTS)
        def _():
            reduce_copy(u, 0).wait_send()

        for stage in (1, 2, 3):
            reduce_copy(u, stage).wait_send()
        for stage in range(4):
            gather_copy(u, stage).wait_send()

        @pl.when((u // 2 != 3) & (u // 2 != 7))
        def _():
            term_copy(u).wait_send()

    for j in range(2):
        z_copy(j).wait_send()


def per_device(tokens, gates, w_gate, w_up, w_down):
    depth = tokens.shape[1]
    ff = w_gate.shape[2]
    cols = 2 * ff
    half = SEG // 2
    bf16 = jnp.bfloat16
    anywhere = pl.BlockSpec(memory_space=pl.ANY)
    vmem = pl.BlockSpec(memory_space=pltpu.VMEM)
    dma = pltpu.SemaphoreType.DMA
    return pl.pallas_call(
        kernel,
        out_shape=jax.ShapeDtypeStruct(tokens.shape, bf16),
        in_specs=[vmem, anywhere, anywhere, anywhere, anywhere],
        out_specs=vmem,
        scratch_shapes=[
            pltpu.VMEM((8, 8, 128), jnp.float32),
            pltpu.VMEM((UNITS * SUB, EXPERTS * SUB), bf16),
            pltpu.VMEM((EXPERTS, depth, cols), bf16),
            pltpu.VMEM((SLOTS, half, cols), bf16),
            pltpu.VMEM((UNITS, half, cols), bf16),
            pltpu.VMEM((UNITS, half // 2, cols), bf16),
            pltpu.VMEM((UNITS, half // 4, cols), bf16),
            pltpu.VMEM((UNITS, half // 8, cols), bf16),
            pltpu.VMEM((UNITS, cols // TILE, depth, TILE), bf16),
            pltpu.VMEM(w_down.shape, bf16),
            pltpu.VMEM((UNITS, SEG, depth), bf16),
            pltpu.VMEM((UNITS, SEG, ff), bf16),
            pltpu.VMEM((UNITS, SEG, depth), bf16),
            pltpu.VMEM((UNITS, SEG, depth), bf16),
            pltpu.VMEM((2, SEG, depth), bf16),
            pltpu.VMEM((2, SEG, depth), bf16),
            dma((2, depth // SUB)),
            dma((3,)),
            dma((8,)),
            dma((8,)),
            dma((8,)),
            dma((8,)),
            dma((4, UNITS)),
            dma((4, UNITS)),
            dma((4, UNITS)),
            dma((4, UNITS)),
            dma((UNITS,)),
            dma((UNITS,)),
            dma((2,)),
            dma((2,)),
        ],
        compiler_params=pltpu.CompilerParams(
            collective_id=0, has_side_effects=True, vmem_limit_bytes=61 * 2**20
        ),
        cost_estimate=pl.CostEstimate(flops=2 * 2**33, bytes_accessed=12 * 2**20, transcendentals=0),
    )(gates, tokens, w_gate, w_up, w_down)


def solution(mesh):
    return jax.shard_map(
        per_device,
        mesh=mesh,
        in_specs=(
            P("blk", "width"),
            P("blk", None),
            P(None, "width", "blk"),
            P(None, "width", "blk"),
            P(None, "blk", "width"),
        ),
        out_specs=P("blk", "width"),
        check_vma=False,
    )
```

```python
import functools
import jax
import jax.numpy as jnp
from jax import lax
from jax.experimental import pallas as pl
from jax.experimental.pallas import tpu as pltpu
from jax.sharding import PartitionSpec as P

SEG = 256
EXPERTS = 8
UNITS = 16
SUB = 32
TILE = 256
SLOTS = 4
MESH = pl.DeviceIdType.MESH
OFFSETS = (0, 1, 6, 9, 12, 15, 18, 20, 21)


def kernel(
    gates_ref, tokens_ref, wg_ref, wu_ref, wd_ref, out_ref,
    gbuf, kmat, keep, psend, precv, r1, r2, r3, merged, wdn, tok, hid, term, yrecv, zsend, zrecv,
    w_sem, l_sem, g_s, g_r, tok_s, tok_r, rs_s, rs_r, ag_s, ag_r, t_s, t_r, z_s, z_r,
):
    depth = tokens_ref.shape[1]
    ff = wg_ref.shape[2]
    cols = 2 * ff
    half, quarter, eighth, share = SEG // 2, SEG // 4, SEG // 8, SEG // 16

    w = lax.axis_index("width")
    b = lax.axis_index("blk")
    core = lax.rem(w, 2)
    x = lax.rem(w // 2, 4)
    zh = w // 8
    y = lax.rem(b, 4)
    zl = b // 4

    bit_a, bit_b = lax.rem((x + 1) // 2, 2), x // 2
    w_pair = w + 1 - 2 * core
    w_a = (zh * 4 + x + 1 - 2 * lax.rem(x, 2)) * 2 + core
    w_b = (zh * 4 + 3 - x) * 2 + core
    w_z = ((1 - zh) * 4 + x) * 2 + core
    b_z = (1 - zl) * 4 + y

    def mul(value, by):
        return pl.multiple_of(value, by)

    def dim(u, place):
        d = lax.rem(u + place, 3)
        e0, e1, e2 = (2 - d) * (1 - d) // 2, d * (2 - d), d * (d - 1) // 2
        return e0 * bit_a + e1 * bit_b + e2 * zh, e0 * w_a + e1 * w_b + e2 * w_z

    def place_of(u):
        r, j = u // 2, lax.rem(u, 2)
        q = lax.rem(r, 4)
        dy = lax.rem(2 + 3 * q + 3 * (q // 2) + 2 * (q // 3), 4)
        dz = lax.rem((r + 1) // 4, 2)
        zo = zl + dz - 2 * zl * dz
        owner = zo * 4 + lax.rem(y + dy, 4)
        return dy, owner, owner * 2 + j

    def rcopy(src, dst, send, recv, device):
        return pltpu.make_async_remote_copy(
            src_ref=src, dst_ref=dst, send_sem=send, recv_sem=recv, device_id=device, device_id_type=MESH
        )

    def weight_copies(i):
        rows = pl.ds(mul(i * SUB, SUB), SUB)
        return (
            pltpu.make_async_copy(wg_ref.at[:, rows, :], keep.at[:, rows, pl.ds(0, ff)], w_sem.at[0, i]),
            pltpu.make_async_copy(wu_ref.at[:, rows, :], keep.at[:, rows, pl.ds(ff, ff)], w_sem.at[1, i]),
        )

    own_tok = [
        pltpu.make_async_copy(tokens_ref.at[pl.ds(j * SEG, SEG), :], tok.at[2 * b + j], l_sem.at[j])
        for j in range(2)
    ]
    down_copy = pltpu.make_async_copy(wd_ref, wdn, l_sem.at[2])

    for copy in own_tok:
        copy.start()

    @pl.loop(0, depth // SUB)
    def _(i):
        for copy in weight_copies(i):
            copy.start()

    down_copy.start()

    gbuf[b] = jnp.zeros((8, 128), jnp.float32)
    gbuf[b, 0:2, 0:EXPERTS] = gates_ref[...]

    barrier = pltpu.get_barrier_semaphore()
    for partner in (w_pair, w_a, w_b, w_z):
        pl.semaphore_signal(barrier, inc=1, device_id=(b, partner), device_id_type=MESH)
    for p in range(1, 8):
        pl.semaphore_signal(barrier, inc=1, device_id=(lax.rem(b + p, 8), w), device_id_type=MESH)
    pl.semaphore_wait(barrier, 11)

    def gate_copy(p):
        return rcopy(gbuf.at[b], gbuf.at[b], g_s.at[p], g_r.at[p], (lax.rem(b + p, 8), w))

    def gate_arrival(p):
        src = lax.rem(b + 8 - p, 8)
        return rcopy(gbuf.at[src], gbuf.at[src], g_s.at[p], g_r.at[p], (lax.rem(b + p, 8), w))

    for p in range(1, 8):
        gate_copy(p).start()

    def tok_copy(k, source, target):
        block = tok.at[pl.ds(2 * source, 2)]
        return rcopy(block, block, tok_s.at[k], tok_r.at[source], (target, w))

    def y_block(dy):
        return zl * 4 + lax.rem(y + dy, 4)

    for copy in own_tok:
        copy.wait()
    tok_copy(0, b, b_z).start()
    for k, dy in enumerate((2, 3, 1)):
        tok_copy(1 + k, b, y_block(dy)).start()

    for p in range(1, 8):
        gate_arrival(p).wait_recv()
    rows_k, cols_k = UNITS * SUB, EXPERTS * SUB
    shift = SUB.bit_length() - 1
    row = lax.broadcasted_iota(jnp.int32, (rows_k, 64), 0) >> shift
    col = lax.broadcasted_iota(jnp.int32, (rows_k, 64), 1)
    pick_row = ((row >> 1) * 8 + (row & 1) == col).astype(jnp.float32).astype(jnp.bfloat16)
    pick_col = (
        (lax.broadcasted_iota(jnp.int32, (128, cols_k), 1) >> shift)
        == lax.broadcasted_iota(jnp.int32, (128, cols_k), 0)
    ).astype(jnp.float32).astype(jnp.bfloat16)
    weights = gbuf[...].reshape(64, 128).astype(jnp.bfloat16)
    spread = jnp.dot(pick_row, weights, preferred_element_type=jnp.float32).astype(jnp.bfloat16)
    spread = jnp.dot(spread, pick_col, preferred_element_type=jnp.float32)
    same = (lax.broadcasted_iota(jnp.int32, (rows_k, cols_k), 0) & (SUB - 1)) == (
        lax.broadcasted_iota(jnp.int32, (rows_k, cols_k), 1) & (SUB - 1)
    )
    kmat[...] = jnp.where(same, spread, 0.0).astype(jnp.bfloat16)

    @pl.loop(0, depth // SUB)
    def _(i):
        for copy in weight_copies(i):
            copy.wait()
        rows = pl.ds(mul(i * SUB, SUB), SUB)
        for n in range(cols // TILE):
            experts = keep[:, rows, n * TILE : (n + 1) * TILE].reshape(cols_k, TILE)
            total = jnp.dot(kmat[...], experts, preferred_element_type=jnp.float32)
            merged[:, n, rows, :] = total.astype(jnp.bfloat16).reshape(UNITS, SUB, TILE)

        @pl.when(i == 2)
        def _():
            tok_copy(0, b_z, b_z).wait_recv()
            for k, dy in enumerate((2, 3, 1)):
                tok_copy(4 + k, b_z, y_block(dy)).start()

    def kept(u, offset, count):
        return keep.at[u // 2, pl.ds(mul(lax.rem(u, 2) * half + offset, 16), count), :]

    def reduce_copy(u, stage):
        if stage == 0:
            return rcopy(psend.at[lax.rem(u, SLOTS)], precv.at[u], rs_s.at[0, u], rs_r.at[0, u], (b, w_pair))
        (b1, w1), (b2, w2), (b3, w3) = (dim(u, k) for k in range(3))
        if stage == 1:
            return rcopy(kept(u, (1 - b1) * quarter, quarter), r1.at[u], rs_s.at[1, u], rs_r.at[1, u], (b, w1))
        if stage == 2:
            offset = b1 * quarter + (1 - b2) * eighth
            return rcopy(kept(u, offset, eighth), r2.at[u], rs_s.at[2, u], rs_r.at[2, u], (b, w2))
        offset = b1 * quarter + b2 * eighth + (1 - b3) * share
        return rcopy(kept(u, offset, share), r3.at[u], rs_s.at[3, u], rs_r.at[3, u], (b, w3))

    def gather_copy(u, stage):
        (b1, w1), (b2, w2), (b3, w3) = (dim(u, k) for k in range(3))
        offset = core * half
        if stage < 3:
            offset = offset + b1 * quarter
        if stage < 2:
            offset = offset + b2 * eighth
        if stage < 1:
            offset = offset + b3 * share
        count = share << stage
        block = hid.at[u, pl.ds(mul(offset, 16), count), :]
        target = (w3, w2, w1, w_pair)[stage]
        return rcopy(block, block, ag_s.at[stage, u], ag_r.at[stage, u], (b, target))

    def gather_arrival(u, stage):
        (b1, w1), (b2, w2), (b3, w3) = (dim(u, k) for k in range(3))
        offset = core * half if stage < 3 else (1 - core) * half
        if stage < 3:
            offset = offset + (b1 if stage < 2 else 1 - b1) * quarter
        if stage < 2:
            offset = offset + (b2 if stage < 1 else 1 - b2) * eighth
        if stage < 1:
            offset = offset + (1 - b3) * share
        count = share << stage
        block = hid.at[u, pl.ds(mul(offset, 16), count), :]
        target = (w3, w2, w1, w_pair)[stage]
        return rcopy(block, block, ag_s.at[stage, u], ag_r.at[stage, u], (b, target))

    def term_copy(u):
        dy, _, _ = place_of(u)
        return rcopy(term.at[u], yrecv.at[u], t_s.at[0, u], t_r.at[0, u], (y_block(dy), w))

    def relay_copy(u, side):
        rows = pl.ds(side * half, half)
        to = (y_block(1 + 2 * side), w)
        return rcopy(term.at[u, rows, :], yrecv.at[u, rows, :], t_s.at[side, u], t_r.at[side, u], to)

    def f32(block):
        return block.astype(jnp.float32)

    def project(u):
        _, owner, s = place_of(u)

        @pl.when((lax.rem(u, 2) == 0) & (u != 6) & (u != 14))
        def _():
            tok_copy(0, owner, b_z).wait_recv()

        @pl.when(u >= SLOTS)
        def _():
            reduce_copy(u - SLOTS, 0).wait_send()

        rows = jnp.concatenate(
            [tok[s, pl.ds(mul(core * half, half), half), :], tok[s, pl.ds(mul((1 - core) * half, half), half), :]],
            axis=0,
        )
        slot = lax.rem(u, SLOTS)
        mine = pl.ds(mul(lax.rem(u, 2) * half, half), half)
        for n in range(cols // TILE):
            part = jnp.dot(rows, merged[s, n], preferred_element_type=jnp.float32).astype(jnp.bfloat16)
            keep[u // 2, mine, n * TILE : (n + 1) * TILE] = part[:half]
            psend[slot, :, n * TILE : (n + 1) * TILE] = part[half:]
        reduce_copy(u, 0).start()

    def reduce_1(u):
        reduce_copy(u, 0).wait_recv()
        b1, _ = dim(u, 0)
        base = lax.rem(u, 2) * half
        for i in range(quarter // 16):
            offset = (1 - b1) * quarter + i * 16
            at = pl.ds(mul(base + offset, 16), 16)
            total = f32(keep[u // 2, at, :]) + f32(precv[u, pl.ds(mul(offset, 16), 16), :])
            keep[u // 2, at, :] = total.astype(jnp.bfloat16)
        reduce_copy(u, 1).start()

    def reduce_2(u):
        reduce_copy(u, 1).wait_recv()
        (b1, _), (b2, _) = dim(u, 0), dim(u, 1)
        base = lax.rem(u, 2) * half
        for i in range(eighth // 16):
            inner = (1 - b2) * eighth + i * 16
            offset = b1 * quarter + inner
            at = pl.ds(mul(base + offset, 16), 16)
            total = (
                f32(keep[u // 2, at, :])
                + f32(precv[u, pl.ds(mul(offset, 16), 16), :])
                + f32(r1[u, pl.ds(mul(inner, 16), 16), :])
            )
            keep[u // 2, at, :] = total.astype(jnp.bfloat16)
        reduce_copy(u, 2).start()

    def gathered(u, last):
        (b1, _), (b2, _) = dim(u, 0), dim(u, 1)
        base = lax.rem(u, 2) * half
        inner = b2 * eighth + last * share
        offset = b1 * quarter + inner
        return pl.ds(mul(base + offset, 16), 16), (
            f32(keep[u // 2, pl.ds(mul(base + offset, 16), 16), :])
            + f32(precv[u, pl.ds(mul(offset, 16), 16), :])
            + f32(r1[u, pl.ds(mul(inner, 16), 16), :])
            + f32(r2[u, pl.ds(mul(last * share, 16), 16), :])
        )

    def reduce_3(u):
        reduce_copy(u, 2).wait_recv()
        b3, _ = dim(u, 2)
        at, total = gathered(u, 1 - b3)
        keep[u // 2, at, :] = total.astype(jnp.bfloat16)
        reduce_copy(u, 3).start()

    def activate(u):
        reduce_copy(u, 3).wait_recv()
        (b1, _), (b2, _), (b3, _) = (dim(u, k) for k in range(3))
        _, total = gathered(u, b3)
        total = total + f32(r3[u])
        gate, up = total[:, :ff], total[:, ff:]
        value = (gate / (1.0 + jnp.exp(-gate)) * up).astype(jnp.bfloat16)
        offset = core * half + b1 * quarter + b2 * eighth + b3 * share
        hid[u, pl.ds(mul(offset, 16), 16), :] = value
        gather_copy(u, 0).start()

    def spread_on(stage):
        def run(u):
            gather_arrival(u, stage - 1).wait_recv()
            gather_copy(u, stage).start()

        return run

    def finish(u):
        gather_arrival(u, 3).wait_recv()
        dy, _, s = place_of(u)
        down = merged[s, 0:4].reshape(4 * TILE, TILE)[:ff]
        part = jnp.dot(hid[u], down, preferred_element_type=jnp.float32)
        term[u] = part.astype(jnp.bfloat16)

        @pl.when(dy == 2)
        def _():
            for side in range(2):
                relay_copy(u, side).start()

        for side in range(2):
            @pl.when(dy == 1 + 2 * side)
            def _():
                far = u - 2 - 2 * side
                relay_copy(far, side).wait_recv()
                rows = pl.ds(side * half, half)
                total = part[side * half : (side + 1) * half] + f32(yrecv[far, rows, :])
                term[u, rows, :] = total.astype(jnp.bfloat16)
                term_copy(u).start()

    def merge_down(i):
        rows = pl.ds(mul(i * SUB, SUB), SUB)
        experts = wdn[:, rows, :].reshape(cols_k, TILE)
        total = jnp.dot(kmat[...], experts, preferred_element_type=jnp.float32)
        to = pl.ds(mul(lax.rem(i, TILE // SUB) * SUB, SUB), SUB)
        merged[:, i // (TILE // SUB), to, :] = total.astype(jnp.bfloat16).reshape(UNITS, SUB, TILE)

    def z_copy(j):
        return rcopy(zsend.at[j], zrecv.at[j], z_s.at[j], z_r.at[j], (b_z, w))

    def send_z():
        for j in range(2):
            total = f32(term[6 + j])
            for r in (5, 6):
                term_copy(2 * r + j).wait_recv()
                total = total + f32(yrecv[2 * r + j])
            zsend[j] = total.astype(jnp.bfloat16)
            z_copy(j).start()

    stages = (
        project, reduce_1, reduce_2, reduce_3, activate,
        spread_on(1), spread_on(2), spread_on(3), finish,
    )
    down_steps = OFFSETS[8] - UNITS
    per_step = -(-(ff // SUB) // down_steps)

    @pl.loop(0, UNITS + OFFSETS[8])
    def _(t):
        for stage, offset in zip(stages, OFFSETS):
            @pl.when((t >= offset) & (t < offset + UNITS))
            def _():
                stage(t - offset)

        @pl.when(t == UNITS)
        def _():
            down_copy.wait()

        @pl.when((t >= UNITS) & (t < OFFSETS[8]))
        def _():
            @pl.loop(0, per_step)
            def _(k):
                i = (t - UNITS) * per_step + k

                @pl.when(i < ff // SUB)
                def _():
                    merge_down(i)

    send_z()

    for j in range(2):
        total = f32(term[14 + j])
        for r in (1, 2):
            term_copy(2 * r + j).wait_recv()
            total = total + f32(yrecv[2 * r + j])
        z_copy(j).wait_recv()
        total = total + f32(zrecv[j])
        out_ref[j * SEG : (j + 1) * SEG, :] = total.astype(jnp.bfloat16)

    for p in range(1, 8):
        gate_copy(p).wait_send()
    tok_copy(0, b, b_z).wait_send()
    for k, dy in enumerate((2, 3, 1)):
        tok_copy(1 + k, b, y_block(dy)).wait_send()
        tok_copy(4 + k, b_z, y_block(dy)).wait_send()

    @pl.loop(0, UNITS)
    def _(u):
        @pl.when(u >= UNITS - SLOTS)
        def _():
            reduce_copy(u, 0).wait_send()

        for stage in (1, 2, 3):
            reduce_copy(u, stage).wait_send()
        for stage in range(4):
            gather_copy(u, stage).wait_send()

        q = lax.rem(u // 2, 4)

        @pl.when(q == 0)
        def _():
            for side in range(2):
                relay_copy(u, side).wait_send()

        @pl.when((q == 1) | (q == 2))
        def _():
            term_copy(u).wait_send()

    for j in range(2):
        z_copy(j).wait_send()


def per_device(tokens, gates, w_gate, w_up, w_down):
    depth = tokens.shape[1]
    ff = w_gate.shape[2]
    cols = 2 * ff
    half = SEG // 2
    bf16 = jnp.bfloat16
    anywhere = pl.BlockSpec(memory_space=pl.ANY)
    vmem = pl.BlockSpec(memory_space=pltpu.VMEM)
    dma = pltpu.SemaphoreType.DMA
    return pl.pallas_call(
        kernel,
        out_shape=jax.ShapeDtypeStruct(tokens.shape, bf16),
        in_specs=[vmem, anywhere, anywhere, anywhere, anywhere],
        out_specs=vmem,
        scratch_shapes=[
            pltpu.VMEM((8, 8, 128), jnp.float32),
            pltpu.VMEM((UNITS * SUB, EXPERTS * SUB), bf16),
            pltpu.VMEM((EXPERTS, depth, cols), bf16),
            pltpu.VMEM((SLOTS, half, cols), bf16),
            pltpu.VMEM((UNITS, half, cols), bf16),
            pltpu.VMEM((UNITS, half // 2, cols), bf16),
            pltpu.VMEM((UNITS, half // 4, cols), bf16),
            pltpu.VMEM((UNITS, half // 8, cols), bf16),
            pltpu.VMEM((UNITS, cols // TILE, depth, TILE), bf16),
            pltpu.VMEM(w_down.shape, bf16),
            pltpu.VMEM((UNITS, SEG, depth), bf16),
            pltpu.VMEM((UNITS, SEG, ff), bf16),
            pltpu.VMEM((UNITS, SEG, depth), bf16),
            pltpu.VMEM((UNITS, SEG, depth), bf16),
            pltpu.VMEM((2, SEG, depth), bf16),
            pltpu.VMEM((2, SEG, depth), bf16),
            dma((2, depth // SUB)),
            dma((3,)),
            dma((8,)),
            dma((8,)),
            dma((8,)),
            dma((8,)),
            dma((4, UNITS)),
            dma((4, UNITS)),
            dma((4, UNITS)),
            dma((4, UNITS)),
            dma((2, UNITS)),
            dma((2, UNITS)),
            dma((2,)),
            dma((2,)),
        ],
        compiler_params=pltpu.CompilerParams(
            collective_id=0, has_side_effects=True, vmem_limit_bytes=61 * 2**20
        ),
        cost_estimate=pl.CostEstimate(flops=2 * 2**33, bytes_accessed=12 * 2**20, transcendentals=0),
    )(gates, tokens, w_gate, w_up, w_down)


def solution(mesh):
    return jax.shard_map(
        per_device,
        mesh=mesh,
        in_specs=(
            P("blk", "width"),
            P("blk", None),
            P(None, "width", "blk"),
            P(None, "width", "blk"),
            P(None, "blk", "width"),
        ),
        out_specs=P("blk", "width"),
        check_vma=False,
    )
```

```python
import functools
import jax
import jax.numpy as jnp
from jax import lax
from jax.experimental import pallas as pl
from jax.experimental.pallas import tpu as pltpu
from jax.sharding import PartitionSpec as P

SEG = 256
EXPERTS = 8
UNITS = 16
SUB = 32
TILE = 256
SLOTS = 4
MESH = pl.DeviceIdType.MESH
OFFSETS = (0, 1, 8, 12, 15, 18, 22, 27, 28)


def kernel(
    gates_ref, tokens_ref, wg_ref, wu_ref, wd_ref, out_ref,
    gbuf, kmat, keep, psend, precv, r1, r2, r3, merged, wdn, tok, hid, term, yrecv, zsend, zrecv,
    w_sem, l_sem, g_s, g_r, tok_s, tok_r, rs_s, rs_r, ag_s, ag_r, t_s, t_r, z_s, z_r,
):
    depth = tokens_ref.shape[1]
    ff = wg_ref.shape[2]
    cols = 2 * ff
    half, quarter, eighth, share = SEG // 2, SEG // 4, SEG // 8, SEG // 16

    w = lax.axis_index("width")
    b = lax.axis_index("blk")
    core = lax.rem(w, 2)
    x = lax.rem(w // 2, 4)
    zh = w // 8
    y = lax.rem(b, 4)
    zl = b // 4

    bit_a, bit_b = lax.rem((x + 1) // 2, 2), x // 2
    w_pair = w + 1 - 2 * core
    w_a = (zh * 4 + x + 1 - 2 * lax.rem(x, 2)) * 2 + core
    w_b = (zh * 4 + 3 - x) * 2 + core
    w_z = ((1 - zh) * 4 + x) * 2 + core
    b_z = (1 - zl) * 4 + y

    def mul(value, by):
        return pl.multiple_of(value, by)

    def dim(u, place):
        d = lax.rem(u + place, 3)
        e0, e1, e2 = (2 - d) * (1 - d) // 2, d * (2 - d), d * (d - 1) // 2
        return e0 * bit_a + e1 * bit_b + e2 * zh, e0 * w_a + e1 * w_b + e2 * w_z

    def place_of(u):
        r, j = u // 2, lax.rem(u, 2)
        q = lax.rem(r, 4)
        dy = lax.rem(1 + 2 * q + q // 2, 4)
        dz = lax.rem((r + 1) // 4, 2)
        zo = zl + dz - 2 * zl * dz
        owner = zo * 4 + lax.rem(y + dy, 4)
        return dy, owner, owner * 2 + j

    def rcopy(src, dst, send, recv, device):
        return pltpu.make_async_remote_copy(
            src_ref=src, dst_ref=dst, send_sem=send, recv_sem=recv, device_id=device, device_id_type=MESH
        )

    def weight_copies(i):
        rows = pl.ds(mul(i * SUB, SUB), SUB)
        return (
            pltpu.make_async_copy(wg_ref.at[:, rows, :], keep.at[:, rows, pl.ds(0, ff)], w_sem.at[0, i]),
            pltpu.make_async_copy(wu_ref.at[:, rows, :], keep.at[:, rows, pl.ds(ff, ff)], w_sem.at[1, i]),
        )

    own_tok = [
        pltpu.make_async_copy(tokens_ref.at[pl.ds(j * SEG, SEG), :], tok.at[2 * b + j], l_sem.at[j])
        for j in range(2)
    ]
    down_copy = pltpu.make_async_copy(wd_ref, wdn, l_sem.at[2])

    for copy in own_tok:
        copy.start()

    @pl.loop(0, depth // SUB)
    def _(i):
        for copy in weight_copies(i):
            copy.start()

    down_copy.start()

    gbuf[b] = jnp.zeros((8, 128), jnp.float32)
    gbuf[b, 0:2, 0:EXPERTS] = gates_ref[...]

    barrier = pltpu.get_barrier_semaphore()
    for partner in (w_pair, w_a, w_b, w_z):
        pl.semaphore_signal(barrier, inc=1, device_id=(b, partner), device_id_type=MESH)
    for p in range(1, 8):
        pl.semaphore_signal(barrier, inc=1, device_id=(lax.rem(b + p, 8), w), device_id_type=MESH)
    pl.semaphore_wait(barrier, 11)

    def gate_copy(p):
        return rcopy(gbuf.at[b], gbuf.at[b], g_s.at[p], g_r.at[p], (lax.rem(b + p, 8), w))

    def gate_arrival(p):
        src = lax.rem(b + 8 - p, 8)
        return rcopy(gbuf.at[src], gbuf.at[src], g_s.at[p], g_r.at[p], (lax.rem(b + p, 8), w))

    for p in range(1, 8):
        gate_copy(p).start()

    def tok_copy(k, source, target):
        block = tok.at[pl.ds(2 * source, 2)]
        return rcopy(block, block, tok_s.at[k], tok_r.at[source], (target, w))

    def y_block(dy):
        return zl * 4 + lax.rem(y + dy, 4)

    for copy in own_tok:
        copy.wait()
    tok_copy(0, b, b_z).start()
    for k, dy in enumerate((3, 1, 2)):
        tok_copy(1 + k, b, y_block(dy)).start()

    for p in range(1, 8):
        gate_arrival(p).wait_recv()
    rows_k, cols_k = UNITS * SUB, EXPERTS * SUB
    shift = SUB.bit_length() - 1
    row = lax.broadcasted_iota(jnp.int32, (rows_k, 64), 0) >> shift
    col = lax.broadcasted_iota(jnp.int32, (rows_k, 64), 1)
    pick_row = ((row >> 1) * 8 + (row & 1) == col).astype(jnp.float32).astype(jnp.bfloat16)
    pick_col = (
        (lax.broadcasted_iota(jnp.int32, (128, cols_k), 1) >> shift)
        == lax.broadcasted_iota(jnp.int32, (128, cols_k), 0)
    ).astype(jnp.float32).astype(jnp.bfloat16)
    weights = gbuf[...].reshape(64, 128).astype(jnp.bfloat16)
    spread = jnp.dot(pick_row, weights, preferred_element_type=jnp.float32).astype(jnp.bfloat16)
    spread = jnp.dot(spread, pick_col, preferred_element_type=jnp.float32)
    same = (lax.broadcasted_iota(jnp.int32, (rows_k, cols_k), 0) & (SUB - 1)) == (
        lax.broadcasted_iota(jnp.int32, (rows_k, cols_k), 1) & (SUB - 1)
    )
    kmat[...] = jnp.where(same, spread, 0.0).astype(jnp.bfloat16)

    @pl.loop(0, depth // SUB)
    def _(i):
        for copy in weight_copies(i):
            copy.wait()
        rows = pl.ds(mul(i * SUB, SUB), SUB)
        for n in range(cols // TILE):
            experts = keep[:, rows, n * TILE : (n + 1) * TILE].reshape(cols_k, TILE)
            total = jnp.dot(kmat[...], experts, preferred_element_type=jnp.float32)
            merged[:, n, rows, :] = total.astype(jnp.bfloat16).reshape(UNITS, SUB, TILE)

    tok_copy(0, b_z, b_z).wait_recv()
    for k, dy in enumerate((3, 1, 2)):
        tok_copy(4 + k, b_z, y_block(dy)).start()

    def kept(u, offset, count):
        return keep.at[u // 2, pl.ds(mul(lax.rem(u, 2) * half + offset, 16), count), :]

    def reduce_copy(u, stage):
        if stage == 0:
            return rcopy(psend.at[lax.rem(u, SLOTS)], precv.at[u], rs_s.at[0, u], rs_r.at[0, u], (b, w_pair))
        (b1, w1), (b2, w2), (b3, w3) = (dim(u, k) for k in range(3))
        if stage == 1:
            return rcopy(kept(u, (1 - b1) * quarter, quarter), r1.at[u], rs_s.at[1, u], rs_r.at[1, u], (b, w1))
        if stage == 2:
            offset = b1 * quarter + (1 - b2) * eighth
            return rcopy(kept(u, offset, eighth), r2.at[u], rs_s.at[2, u], rs_r.at[2, u], (b, w2))
        offset = b1 * quarter + b2 * eighth + (1 - b3) * share
        return rcopy(kept(u, offset, share), r3.at[u], rs_s.at[3, u], rs_r.at[3, u], (b, w3))

    def gather_copy(u, stage):
        (b1, w1), (b2, w2), (b3, w3) = (dim(u, k) for k in range(3))
        offset = core * half
        if stage < 3:
            offset = offset + b1 * quarter
        if stage < 2:
            offset = offset + b2 * eighth
        if stage < 1:
            offset = offset + b3 * share
        count = share << stage
        block = hid.at[u, pl.ds(mul(offset, 16), count), :]
        target = (w3, w2, w1, w_pair)[stage]
        return rcopy(block, block, ag_s.at[stage, u], ag_r.at[stage, u], (b, target))

    def gather_arrival(u, stage):
        (b1, w1), (b2, w2), (b3, w3) = (dim(u, k) for k in range(3))
        offset = core * half if stage < 3 else (1 - core) * half
        if stage < 3:
            offset = offset + (b1 if stage < 2 else 1 - b1) * quarter
        if stage < 2:
            offset = offset + (b2 if stage < 1 else 1 - b2) * eighth
        if stage < 1:
            offset = offset + (1 - b3) * share
        count = share << stage
        block = hid.at[u, pl.ds(mul(offset, 16), count), :]
        target = (w3, w2, w1, w_pair)[stage]
        return rcopy(block, block, ag_s.at[stage, u], ag_r.at[stage, u], (b, target))

    def term_copy(u):
        dy, owner, _ = place_of(u)
        return rcopy(term.at[u], yrecv.at[u], t_s.at[u], t_r.at[u], (y_block(dy), w))

    def f32(block):
        return block.astype(jnp.float32)

    def project(u):
        _, owner, s = place_of(u)

        @pl.when((lax.rem(u, 2) == 0) & (u != 6) & (u != 14))
        def _():
            tok_copy(0, owner, b_z).wait_recv()

        @pl.when(u >= SLOTS)
        def _():
            reduce_copy(u - SLOTS, 0).wait_send()

        rows = jnp.concatenate(
            [tok[s, pl.ds(mul(core * half, half), half), :], tok[s, pl.ds(mul((1 - core) * half, half), half), :]],
            axis=0,
        )
        slot = lax.rem(u, SLOTS)
        mine = pl.ds(mul(lax.rem(u, 2) * half, half), half)
        for n in range(cols // TILE):
            part = jnp.dot(rows, merged[s, n], preferred_element_type=jnp.float32).astype(jnp.bfloat16)
            keep[u // 2, mine, n * TILE : (n + 1) * TILE] = part[:half]
            psend[slot, :, n * TILE : (n + 1) * TILE] = part[half:]
        reduce_copy(u, 0).start()

    def reduce_1(u):
        reduce_copy(u, 0).wait_recv()
        b1, _ = dim(u, 0)
        base = lax.rem(u, 2) * half
        for i in range(quarter // 16):
            offset = (1 - b1) * quarter + i * 16
            at = pl.ds(mul(base + offset, 16), 16)
            total = f32(keep[u // 2, at, :]) + f32(precv[u, pl.ds(mul(offset, 16), 16), :])
            keep[u // 2, at, :] = total.astype(jnp.bfloat16)
        reduce_copy(u, 1).start()

    def reduce_2(u):
        reduce_copy(u, 1).wait_recv()
        (b1, _), (b2, _) = dim(u, 0), dim(u, 1)
        base = lax.rem(u, 2) * half
        for i in range(eighth // 16):
            inner = (1 - b2) * eighth + i * 16
            offset = b1 * quarter + inner
            at = pl.ds(mul(base + offset, 16), 16)
            total = (
                f32(keep[u // 2, at, :])
                + f32(precv[u, pl.ds(mul(offset, 16), 16), :])
                + f32(r1[u, pl.ds(mul(inner, 16), 16), :])
            )
            keep[u // 2, at, :] = total.astype(jnp.bfloat16)
        reduce_copy(u, 2).start()

    def gathered(u, last):
        (b1, _), (b2, _) = dim(u, 0), dim(u, 1)
        base = lax.rem(u, 2) * half
        inner = b2 * eighth + last * share
        offset = b1 * quarter + inner
        return pl.ds(mul(base + offset, 16), 16), (
            f32(keep[u // 2, pl.ds(mul(base + offset, 16), 16), :])
            + f32(precv[u, pl.ds(mul(offset, 16), 16), :])
            + f32(r1[u, pl.ds(mul(inner, 16), 16), :])
            + f32(r2[u, pl.ds(mul(last * share, 16), 16), :])
        )

    def reduce_3(u):
        reduce_copy(u, 2).wait_recv()
        b3, _ = dim(u, 2)
        at, total = gathered(u, 1 - b3)
        keep[u // 2, at, :] = total.astype(jnp.bfloat16)
        reduce_copy(u, 3).start()

    def activate(u):
        reduce_copy(u, 3).wait_recv()
        (b1, _), (b2, _), (b3, _) = (dim(u, k) for k in range(3))
        _, total = gathered(u, b3)
        total = total + f32(r3[u])
        gate, up = total[:, :ff], total[:, ff:]
        value = (gate / (1.0 + jnp.exp(-gate)) * up).astype(jnp.bfloat16)
        offset = core * half + b1 * quarter + b2 * eighth + b3 * share
        hid[u, pl.ds(mul(offset, 16), 16), :] = value
        gather_copy(u, 0).start()

    def spread_on(stage):
        def run(u):
            gather_arrival(u, stage - 1).wait_recv()
            gather_copy(u, stage).start()

        return run

    def finish(u):
        gather_arrival(u, 3).wait_recv()
        dy, _, s = place_of(u)
        down = merged[s, 0:4].reshape(4 * TILE, TILE)[:ff]
        part = jnp.dot(hid[u], down, preferred_element_type=jnp.float32)
        term[u] = part.astype(jnp.bfloat16)

        @pl.when(dy != 0)
        def _():
            term_copy(u).start()

    def merge_down(i):
        rows = pl.ds(mul(i * SUB, SUB), SUB)
        experts = wdn[:, rows, :].reshape(cols_k, TILE)
        total = jnp.dot(kmat[...], experts, preferred_element_type=jnp.float32)
        to = pl.ds(mul(lax.rem(i, TILE // SUB) * SUB, SUB), SUB)
        merged[:, i // (TILE // SUB), to, :] = total.astype(jnp.bfloat16).reshape(UNITS, SUB, TILE)

    def z_copy(j):
        return rcopy(zsend.at[j], zrecv.at[j], z_s.at[j], z_r.at[j], (b_z, w))

    def send_z():
        for j in range(2):
            total = f32(term[6 + j])
            for r in (4, 5, 6):
                term_copy(2 * r + j).wait_recv()
                total = total + f32(yrecv[2 * r + j])
            zsend[j] = total.astype(jnp.bfloat16)
            z_copy(j).start()

    stages = (
        project, reduce_1, reduce_2, reduce_3, activate,
        spread_on(1), spread_on(2), spread_on(3), finish,
    )
    down_steps = OFFSETS[8] - UNITS
    per_step = -(-(ff // SUB) // down_steps)

    @pl.loop(0, UNITS + OFFSETS[8])
    def _(t):
        for stage, offset in zip(stages, OFFSETS):
            @pl.when((t >= offset) & (t < offset + UNITS))
            def _():
                stage(t - offset)

        @pl.when(t == UNITS)
        def _():
            down_copy.wait()

        @pl.when((t >= UNITS) & (t < OFFSETS[8]))
        def _():
            @pl.loop(0, per_step)
            def _(k):
                i = (t - UNITS) * per_step + k

                @pl.when(i < ff // SUB)
                def _():
                    merge_down(i)

        @pl.when(t == OFFSETS[8] + 14)
        def _():
            send_z()

    for j in range(2):
        total = f32(term[14 + j])
        for r in (0, 1, 2):
            term_copy(2 * r + j).wait_recv()
            total = total + f32(yrecv[2 * r + j])
        z_copy(j).wait_recv()
        total = total + f32(zrecv[j])
        out_ref[j * SEG : (j + 1) * SEG, :] = total.astype(jnp.bfloat16)

    for p in range(1, 8):
        gate_copy(p).wait_send()
    tok_copy(0, b, b_z).wait_send()
    for k, dy in enumerate((3, 1, 2)):
        tok_copy(1 + k, b, y_block(dy)).wait_send()
        tok_copy(4 + k, b_z, y_block(dy)).wait_send()

    @pl.loop(0, UNITS)
    def _(u):
        @pl.when(u >= UNITS - SLOTS)
        def _():
            reduce_copy(u, 0).wait_send()

        for stage in (1, 2, 3):
            reduce_copy(u, stage).wait_send()
        for stage in range(4):
            gather_copy(u, stage).wait_send()

        @pl.when((u // 2 != 3) & (u // 2 != 7))
        def _():
            term_copy(u).wait_send()

    for j in range(2):
        z_copy(j).wait_send()


def per_device(tokens, gates, w_gate, w_up, w_down):
    depth = tokens.shape[1]
    ff = w_gate.shape[2]
    cols = 2 * ff
    half = SEG // 2
    bf16 = jnp.bfloat16
    anywhere = pl.BlockSpec(memory_space=pl.ANY)
    vmem = pl.BlockSpec(memory_space=pltpu.VMEM)
    dma = pltpu.SemaphoreType.DMA
    return pl.pallas_call(
        kernel,
        out_shape=jax.ShapeDtypeStruct(tokens.shape, bf16),
        in_specs=[vmem, anywhere, anywhere, anywhere, anywhere],
        out_specs=vmem,
        scratch_shapes=[
            pltpu.VMEM((8, 8, 128), jnp.float32),
            pltpu.VMEM((UNITS * SUB, EXPERTS * SUB), bf16),
            pltpu.VMEM((EXPERTS, depth, cols), bf16),
            pltpu.VMEM((SLOTS, half, cols), bf16),
            pltpu.VMEM((UNITS, half, cols), bf16),
            pltpu.VMEM((UNITS, half // 2, cols), bf16),
            pltpu.VMEM((UNITS, half // 4, cols), bf16),
            pltpu.VMEM((UNITS, half // 8, cols), bf16),
            pltpu.VMEM((UNITS, cols // TILE, depth, TILE), bf16),
            pltpu.VMEM(w_down.shape, bf16),
            pltpu.VMEM((UNITS, SEG, depth), bf16),
            pltpu.VMEM((UNITS, SEG, ff), bf16),
            pltpu.VMEM((UNITS, SEG, depth), bf16),
            pltpu.VMEM((UNITS, SEG, depth), bf16),
            pltpu.VMEM((2, SEG, depth), bf16),
            pltpu.VMEM((2, SEG, depth), bf16),
            dma((2, depth // SUB)),
            dma((3,)),
            dma((8,)),
            dma((8,)),
            dma((8,)),
            dma((8,)),
            dma((4, UNITS)),
            dma((4, UNITS)),
            dma((4, UNITS)),
            dma((4, UNITS)),
            dma((UNITS,)),
            dma((UNITS,)),
            dma((2,)),
            dma((2,)),
        ],
        compiler_params=pltpu.CompilerParams(
            collective_id=0, has_side_effects=True, vmem_limit_bytes=61 * 2**20
        ),
        cost_estimate=pl.CostEstimate(flops=2 * 2**33, bytes_accessed=12 * 2**20, transcendentals=0),
    )(gates, tokens, w_gate, w_up, w_down)


def solution(mesh):
    return jax.shard_map(
        per_device,
        mesh=mesh,
        in_specs=(
            P("blk", "width"),
            P("blk", None),
            P(None, "width", "blk"),
            P(None, "width", "blk"),
            P(None, "blk", "width"),
        ),
        out_specs=P("blk", "width"),
        check_vma=False,
    )
```
